512 devices in a mesh: grid: 128 (over x, z, y_hi, core), state: 4 (over y_lo).
Axes of the slice: x: 4, y: 8 (y_hi: 2, y_lo: 4; y = y_hi * 4 + y_lo), z: 8, core: 2. Of those that a mesh axis runs over, the one named last changes fastest.
Arguments:
- x_block: float32 [262144, 512], P('grid', 'state'), as said below
- h_block: float32 [262144, 512], P('grid', 'state'), as said below
- mass_weights: float32 [262144], P('grid'), as said below
- coefficients: float32 [512, 512], P(None, 'state'), may hold values from -0.25 to 0.25
Outputs:
- rotated: float32 [262144, 512], P('grid', 'state')
- projected: float32 [512, 512], P(None, 'state')
The draws below stay inside these ranges and needn't reach their ends.
Inputs may be any that keep to these rules, and one draw needn't show every extreme that they name: x_block is a real field whose columns are correlated with their neighbours so that gram is positive definite. h_block's values are of the magnitude of x_block's. `mass_weights`: positive weights of order 1 / 262144.
All inputs are finite; a program needn't handle non-finite values.
Results may differ from the reference program's by a relative error of at most 0.00024.
Values sent between devices are 32-bit elements; how exact they have to be, the bound alone decides.
No kernel may reach another device: no remote copies, remote signals or barrier semaphores. Data moves between devices by JAX's collectives and lax.ppermute only.
A program may use at most 64 MiB of HBM per device.

```python
import math
import jax
import jax.numpy as jnp
from jax import lax

NB = 512
NPTS = 262144


def make_block(key):
    first_key = jax.random.fold_in(jax.random.fold_in(key, 11), 0)
    third_key = jax.random.fold_in(jax.random.fold_in(key, 11), 2)
    normals = jax.random.normal(first_key, (NPTS, NB), jnp.float32)
    mixing = 0.5
    return (normals + mixing * jnp.roll(normals, -1, axis=1), third_key)


def draw_x_block(key, part):
    return make_block(key)[0]


def draw_h_block(key, part):
    states, third_key = make_block(key)
    eps_key, noise_key = jax.random.split(third_key)
    energies = jnp.exp(jax.random.uniform(eps_key, (NPTS, 1), jnp.float32, math.log(0.5), math.log(4.0)))
    noise = jax.random.normal(noise_key, (NPTS, NB), jnp.float32)
    return energies * states + 0.3 * noise


def draw_mass_weights(key, part):
    local_key = jax.random.fold_in(key, 23)
    factors = jnp.exp(jax.random.uniform(local_key, (NPTS,), jnp.float32, math.log(0.5), math.log(2.0)))
    ramp = 1.0 + 2.0 * jnp.arange(NPTS).astype(jnp.float32) / NPTS
    return factors * ramp / NPTS


def block_levels(own_key, shape, cuts, smallest, largest):
    loudness = 1.0
    for dim, parts in cuts:
        steps = jax.random.uniform(jax.random.fold_in(jax.random.fold_in(own_key, 6), dim), (parts,), jnp.float32, smallest / len(cuts), largest / len(cuts))
        loudness = loudness * jnp.repeat(jnp.exp(steps), shape[dim] // parts).reshape((-1,) + (1,) * (len(shape) - 1 - dim))
    return loudness


def gaussian(key, shape, width, bound, shards=(), kind=jnp.bfloat16):
    values = width * jax.random.normal(key, shape, jnp.float32)
    if shards:
        values = values * block_levels(key, shape, shards, -0.22, 0.18)
    return jnp.clip(values, -bound, bound).astype(kind)


def setup_inputs(seed: int = 0) -> dict:
    splits = jax.random.split(jax.random.key(seed), 5)
    x_block = draw_x_block(jax.random.fold_in(splits[4], 71), 0)
    h_block = draw_h_block(jax.random.fold_in(splits[4], 71), 0)
    mass_weights = draw_mass_weights(jax.random.fold_in(splits[4], 71), 0)
    coefficients = gaussian(splits[3], (NB, NB), NB ** -0.5, 0.25, ((1, 4),), jnp.float32)
    return {"x_block": x_block, "h_block": h_block, "mass_weights": mass_weights, "coefficients": coefficients}


def reference(x_block, h_block, mass_weights, coefficients):
    hp = lax.Precision.HIGHEST
    weighted_x = mass_weights[:, None] * x_block
    weighted_h = mass_weights[:, None] * h_block
    gram_matrix = jnp.dot(x_block.T, weighted_x, precision=hp)
    hamil_matrix = jnp.dot(x_block.T, weighted_h, precision=hp)
    factor = jnp.linalg.cholesky(gram_matrix)
    half_solve = lax.linalg.triangular_solve(factor, hamil_matrix, left_side=True, lower=True)
    projected = lax.linalg.triangular_solve(factor, half_solve, left_side=False, lower=True, transpose_a=True)
    rotation = lax.linalg.triangular_solve(factor, coefficients, left_side=True, lower=True, transpose_a=True)
    rotated = jnp.dot(x_block, rotation, precision=hp)
    return (rotated, projected)
```

```python
import jax
import jax.numpy as jnp
from jax import lax
from jax.sharding import Mesh, PartitionSpec as P

GRID = ("x", "z", "yh", "core")
ALL = GRID + ("state",)
SPREAD = ("x", "z", "yh")
HIGHEST = lax.Precision.HIGHEST


def after(value, *earlier):
    return lax.optimization_barrier((value, *earlier))[0]


def exchange(value, axes):
    return lax.all_to_all(value, axes, 0, 0, tiled=True)


def scatter_sum(value, axes):
    count = lax.axis_size(axes)
    got = exchange(value, axes)
    return jnp.sum(got.reshape(count, -1, value.shape[1]), axis=0)


def copies(value, axes):
    count = lax.axis_size(axes)
    return jnp.broadcast_to(value, (count,) + value.shape).reshape(-1, value.shape[1])


def spread(value, axes):
    return exchange(copies(value, axes), axes)


def full_sum(value, axes):
    count = lax.axis_size(axes)
    return jnp.sum(spread(value, axes).reshape(count, -1, value.shape[1]), axis=0)


def shards(x_block, h_block, mass_weights, coefficients):
    own_width = x_block.shape[1]
    state = lax.axis_index("state")
    x_rows = lax.all_to_all(x_block, "state", 0, 1, tiled=True)
    points, nb = x_rows.shape
    weights = lax.dynamic_slice_in_dim(mass_weights, state * points, points, 0)
    weighted_x = weights[:, None] * x_rows
    gram = jnp.dot(x_rows.T, weighted_x, precision=HIGHEST)
    gram = scatter_sum(gram, "core")
    h_rows = lax.all_to_all(after(h_block, x_rows), "state", 0, 1, tiled=True)
    gram = scatter_sum(gram, SPREAD)
    gram = full_sum(gram, "state")
    hamil = jnp.dot(weighted_x.T, after(h_rows, gram), precision=HIGHEST)
    hamil = scatter_sum(hamil, "core")
    gathered = spread(after(x_block, hamil), "state").reshape(-1, x_block.shape[0], own_width)
    gram = spread(gram, SPREAD)
    hamil = scatter_sum(hamil, SPREAD)
    gram = spread(gram, "core")
    hamil = full_sum(hamil, "state")
    hamil = spread(hamil, SPREAD)
    factor = jnp.linalg.cholesky(gram)
    inverse = lax.linalg.triangular_solve(
        factor, jnp.eye(nb, dtype=jnp.float32), left_side=True, lower=True
    )
    rotation = jnp.dot(inverse.T, coefficients, precision=HIGHEST)
    rotated = sum(
        jnp.dot(block, part, precision=HIGHEST)
        for block, part in zip(gathered, rotation.reshape(-1, own_width, own_width))
    )
    hamil = spread(hamil, "core")
    own_inverse = lax.dynamic_slice_in_dim(inverse, state * own_width, own_width, 0)
    half = jnp.dot(hamil, own_inverse.T, precision=HIGHEST)
    projected = jnp.dot(inverse, half, precision=HIGHEST)
    return (rotated, projected)


def solution(mesh):
    split = Mesh(mesh.devices.reshape(4, 8, 2, 2, 4), ALL)
    placed = (P(GRID, "state"), P(GRID, "state"), P(GRID), P(None, "state"))
    return jax.shard_map(
        shards,
        mesh=split,
        in_specs=placed,
        out_specs=(P(GRID, "state"), P(None, "state")),
        check_vma=False,
    )
```

```python
import functools

import jax
import jax.numpy as jnp
from jax import lax
from jax.experimental import pallas as pl
from jax.experimental.pallas import tpu as pltpu
from jax.sharding import Mesh, PartitionSpec as P

GRID = ("x", "z", "yh", "core")
ALL = GRID + ("state",)
PLANE = ("x", "z")
LINE = ("yh", "state")
HIGHEST = lax.Precision.HIGHEST
EDGE, SUB = 128, 8
dot = functools.partial(lax.dot_general, precision=HIGHEST, preferred_element_type=jnp.float32)
PLAIN, BY_ROWS = (((1,), (0,)), ((), ())), (((1,), (1,)), ((), ()))


def after(value, *earlier):
    return lax.optimization_barrier((value, *earlier))[0]


def exchange(value, axes):
    return lax.all_to_all(value, axes, 0, 0, tiled=True)


def total(value, axes):
    return jnp.sum(value.reshape(lax.axis_size(axes), -1, value.shape[1]), axis=0)


def copies(value, axes):
    count = lax.axis_size(axes)
    return jnp.broadcast_to(value, (count,) + value.shape).reshape(-1, value.shape[1])


def block_inverse(rows):
    at_row = lax.broadcasted_iota(jnp.int32, (SUB, EDGE), 0)
    at_lane = lax.broadcasted_iota(jnp.int32, (SUB, EDGE), 1)
    groups = len(rows)
    left = list(rows)
    right = [jnp.where(at_lane == at_row + SUB * g, 1.0, 0.0).astype(jnp.float32) for g in range(groups)]

    def spread_row(value, c):
        return jnp.broadcast_to(value[c : c + 1, :], (SUB, EDGE))

    def spread_col(value, c):
        return jnp.broadcast_to(value[:, c : c + 1], (SUB, EDGE))

    for k in range(groups):
        cols = {g: [spread_col(left[g], SUB * k + c) for c in range(SUB)] for g in range(k, groups)}
        for c in range(SUB):
            scale = lax.rsqrt(spread_row(cols[k][c], c))
            inv = scale * scale
            left_row, right_row = spread_row(left[k], c), spread_row(right[k], c)
            col_row = {d: spread_row(cols[k][d], c) for d in range(c + 1, SUB)}
            for g in range(k, groups):
                factor = cols[g][c] * inv
                if g == k:
                    factor = jnp.where(at_row > c, factor, 0.0)
                for d in range(c + 1, SUB):
                    cols[g][d] = cols[g][d] - factor * col_row[d]
                left[g] = left[g] - factor * left_row
                new = right[g] - factor * right_row
                right[g] = jnp.where(at_row == c, right_row * scale, new) if g == k else new
    return right


def eliminate(first, last, work, out_ref, block):
    nb = work.shape[0]
    at_row = lax.broadcasted_iota(jnp.int32, (nb, EDGE), 0)

    @pl.loop(first, last)
    def _(k):
        start = pl.multiple_of(k * EDGE, EDGE)
        own = pl.ds(start, EDGE)
        rows = [work[pl.ds(pl.multiple_of(start + SUB * g, SUB), SUB), own] for g in range(EDGE // SUB)]
        for g, row in enumerate(block_inverse(rows)):
            block[SUB * g : SUB * (g + 1), :] = row
        inverse = block[...]
        panel = dot(work[:, own], inverse, BY_ROWS)
        panel = jnp.where(at_row >= start + EDGE, panel, 0.0)
        done = dot(inverse, work[own, nb:], PLAIN)
        out_ref[own, :] = done
        work[:, :nb] = work[:, :nb] - dot(panel, panel, BY_ROWS)
        work[:, nb:] = work[:, nb:] - dot(panel, done, PLAIN)


def first_half(gram_ref, work, out_ref, block):
    nb = gram_ref.shape[0]
    work[:, :nb] = gram_ref[...]
    row = lax.broadcasted_iota(jnp.int32, (nb, nb), 0)
    col = lax.broadcasted_iota(jnp.int32, (nb, nb), 1)
    work[:, nb:] = jnp.where(row == col, 1.0, 0.0).astype(jnp.float32)
    out_ref[nb // 2 :, :] = jnp.zeros((nb // 2, nb), jnp.float32)
    eliminate(0, nb // EDGE // 2, work, out_ref, block)


def second_half(work_in, out_in, out_ref, work, block):
    nb = work.shape[0]
    work[...] = work_in[...]
    out_ref[...] = out_in[...]
    eliminate(nb // EDGE // 2, nb // EDGE, work, out_ref, block)


def in_vmem(body, count, out_shape, scratch):
    in_vmem_spec = pl.BlockSpec(memory_space=pltpu.VMEM)
    return pl.pallas_call(
        body,
        out_shape=out_shape,
        in_specs=[in_vmem_spec] * count,
        out_specs=jax.tree.map(lambda _: in_vmem_spec, out_shape),
        scratch_shapes=scratch,
        cost_estimate=pl.CostEstimate(flops=10**10, bytes_accessed=2**22, transcendentals=0),
        compiler_params=pltpu.CompilerParams(vmem_limit_bytes=32 * 2**20),
    )


def shards(x_block, h_block, mass_weights, coefficients):
    own_width = x_block.shape[1]
    state = lax.axis_index("state")
    states = lax.axis_size("state")
    x_rows = lax.all_to_all(x_block, "state", 0, 1, tiled=True)
    points, nb = x_rows.shape
    f32 = functools.partial(jax.ShapeDtypeStruct, dtype=jnp.float32)
    block = pltpu.VMEM((EDGE, EDGE), jnp.float32)
    weights = lax.dynamic_slice_in_dim(mass_weights, state * points, points, 0)
    weighted_x = weights[:, None] * x_rows

    h_mine = after(h_block, x_rows).reshape(states, points, own_width)
    h_parts = []
    for step in range(states):
        part = lax.dynamic_index_in_dim(h_mine, (state + step) % states, 0, keepdims=False)
        if step:
            part = lax.ppermute(part, "state", [(i, (i + step) % states) for i in range(states)])
        h_parts.append(part)
    gathered = lax.all_gather(after(x_block, x_rows), "state", axis=1, tiled=True)

    gram = jnp.dot(x_rows.T, weighted_x, precision=HIGHEST)
    gram = total(exchange(gram, "core"), "core")
    gram = total(exchange(gram, PLANE), PLANE)
    gram = total(exchange(copies(gram, LINE), LINE), LINE)

    products = [dot(weighted_x, part, (((0,), (0,)), ((), ()))) for part in h_parts]
    hamil = jnp.stack(products)
    order = (state - jnp.arange(states)) % states
    hamil = jnp.concatenate([lax.dynamic_index_in_dim(hamil, order[i], 0, keepdims=False) for i in range(states)], axis=1)
    hamil = after(hamil, gram)
    hamil = total(exchange(hamil, "core"), "core")

    parts = lax.axis_size(PLANE)
    both = jnp.concatenate(
        [jnp.broadcast_to(gram, (parts,) + gram.shape), hamil.reshape(parts, -1, nb)], axis=1
    )
    both = exchange(both.reshape(-1, nb), PLANE).reshape(both.shape)
    gram, hamil = both[:, : gram.shape[0]].reshape(-1, nb), jnp.sum(both[:, gram.shape[0] :], axis=0)
    gram = exchange(copies(gram, "core"), "core")
    hamil = exchange(copies(hamil, LINE), LINE)

    work, inverse = in_vmem(first_half, 1, (f32((nb, 2 * nb)), f32((nb, nb))), [block])(gram)
    hamil, work = lax.optimization_barrier((hamil, work))
    hamil = total(hamil, LINE)
    hamil = exchange(copies(hamil, PLANE), PLANE)
    inverse = in_vmem(second_half, 2, f32((nb, nb)), [pltpu.VMEM((nb, 2 * nb), jnp.float32), block])(work, inverse)
    rotation = jnp.dot(inverse.T, coefficients, precision=HIGHEST)
    hamil = exchange(copies(hamil, "core"), "core")
    rotated = jnp.dot(gathered, rotation, precision=lax.Precision.HIGH)
    own_inverse = lax.dynamic_slice_in_dim(inverse, state * own_width, own_width, 0)
    half = jnp.dot(hamil, own_inverse.T, precision=HIGHEST)
    projected = jnp.dot(inverse, half, precision=HIGHEST)
    return (rotated, projected)


def solution(mesh):
    split = Mesh(mesh.devices.reshape(4, 8, 2, 2, 4), ALL)
    placed = (P(GRID, "state"), P(GRID, "state"), P(GRID), P(None, "state"))
    return jax.shard_map(
        shards,
        mesh=split,
        in_specs=placed,
        out_specs=(P(GRID, "state"), P(None, "state")),
        check_vma=False,
    )
```

```python
import functools

import jax
import jax.numpy as jnp
from jax import lax
from jax.experimental import pallas as pl
from jax.experimental.pallas import tpu as pltpu
from jax.sharding import Mesh, PartitionSpec as P

GRID = ("x", "z", "yh", "core")
ALL = GRID + ("state",)
PLANE = ("x", "z")
LINE = ("yh", "state")
HIGHEST = lax.Precision.HIGHEST
EDGE, SUB = 128, 8
dot = functools.partial(lax.dot_general, precision=HIGHEST, preferred_element_type=jnp.float32)
PLAIN, BY_ROWS, BY_COLS = (((1,), (0,)), ((), ())), (((1,), (1,)), ((), ())), (((0,), (0,)), ((), ()))


def after(value, *earlier):
    return lax.optimization_barrier((value, *earlier))[0]


def exchange(value, axes):
    return lax.all_to_all(value, axes, 0, 0, tiled=True)


def total(value, axes):
    return jnp.sum(value.reshape(lax.axis_size(axes), -1, value.shape[1]), axis=0)


def copies(value, axes):
    count = lax.axis_size(axes)
    return jnp.broadcast_to(value, (count,) + value.shape).reshape(-1, value.shape[1])


def block_inverse(rows):
    at_row = lax.broadcasted_iota(jnp.int32, (SUB, EDGE), 0)
    at_lane = lax.broadcasted_iota(jnp.int32, (SUB, EDGE), 1)
    groups = len(rows)
    left = list(rows)
    right = [jnp.where(at_lane == at_row + SUB * g, 1.0, 0.0).astype(jnp.float32) for g in range(groups)]

    def spread_row(value, c):
        return jnp.broadcast_to(value[c : c + 1, :], (SUB, EDGE))

    def spread_col(value, c):
        return jnp.broadcast_to(value[:, c : c + 1], (SUB, EDGE))

    for k in range(groups):
        cols = {g: [spread_col(left[g], SUB * k + c) for c in range(SUB)] for g in range(k, groups)}
        for c in range(SUB):
            scale = lax.rsqrt(spread_row(cols[k][c], c))
            inv = scale * scale
            left_row, right_row = spread_row(left[k], c), spread_row(right[k], c)
            col_row = {d: spread_row(cols[k][d], c) for d in range(c + 1, SUB)}
            below = jnp.where(at_row > c, cols[k][c], 0.0)
            for d in range(c + 1, SUB):
                cols[k][d] = cols[k][d] - (below * col_row[d]) * inv
            left[k] = left[k] - (below * left_row) * inv
            right[k] = jnp.where(at_row == c, right_row * scale, right[k] - (below * right_row) * inv)
            for g in range(k + 1, groups):
                factor = cols[g][c] * inv
                for d in range(c + 1, SUB):
                    cols[g][d] = cols[g][d] - factor * col_row[d]
                left[g] = left[g] - factor * left_row
                right[g] = right[g] - factor * right_row
    return right


def pack(matrix, first_rows):
    return jnp.concatenate(
        [matrix[first:, EDGE * j : EDGE * (j + 1)] for j, first in enumerate(first_rows)], axis=0
    )


def panel_pieces(first_rows, nb, splits):
    pieces, at = [], 0
    for first in first_rows:
        panel, row, end = [], first, at + nb - first
        while at < end:
            (low, high, offset) = next(s for s in splits if s[0] <= at < s[1])
            count = min(end, high) - at
            panel.append((row, count, at - low + offset))
            row, at = row + count, at + count
        pieces.append(panel)
    return pieces


def small_matrices(gram_pieces, hamil_pieces, state_ref, packed, coefficients, rotation_ref, projected_ref, work, inverse, block):
    nb = work.shape[0]
    blocks = nb // EDGE
    work[...] = jnp.zeros((nb, nb), jnp.float32)
    inverse[...] = jnp.zeros((nb, nb), jnp.float32)
    for j, panel in enumerate(gram_pieces):
        for row, count, at in panel:
            work[row : row + count, EDGE * j : EDGE * (j + 1)] = packed[at : at + count, :]

    @pl.loop(0, blocks)
    def _(k):
        start = pl.multiple_of(k * EDGE, EDGE)
        rows = [
            work[pl.ds(pl.multiple_of(start + SUB * g, SUB), SUB), pl.ds(start, EDGE)]
            for g in range(EDGE // SUB)
        ]
        for g, row in enumerate(block_inverse(rows)):
            block[SUB * g : SUB * (g + 1), :] = row

        for j in range(blocks):

            @pl.when(k == j)
            def _():
                low, high = EDGE * j, EDGE * (j + 1)
                inverse[low:high, low:high] = block[...]
                if j + 1 < blocks:
                    panel = dot(work[high:, low:high], block[...], BY_ROWS)
                    work[high:, high:] = work[high:, high:] - dot(panel, panel, BY_ROWS)
                if j:
                    inverse[low:high, :low] = dot(block[...], inverse[low:high, :low], PLAIN)
                if j + 1 < blocks:
                    inverse[high:, :high] = inverse[high:, :high] - dot(panel, inverse[low:high, :high], PLAIN)

    for j in range(blocks):
        low, high = EDGE * j, EDGE * (j + 1)
        rotation_ref[low:high, :] = dot(inverse[low:, low:high], coefficients[low:, :], BY_COLS)
    own = pl.ds(pl.multiple_of(state_ref[0] * EDGE, EDGE), EDGE)
    half = jnp.zeros((nb, EDGE), jnp.float32)
    for j, panel in enumerate(hamil_pieces):
        columns = jnp.concatenate([packed[at : at + count, :] for _, count, at in panel], axis=0)
        half = half + dot(columns, inverse[own, EDGE * j : EDGE * (j + 1)], BY_ROWS)
    for j in range(blocks):
        high = EDGE * (j + 1)
        projected_ref[high - EDGE : high, :] = dot(inverse[high - EDGE : high, :high], half[:high], PLAIN)


def solve(state, packed, coefficients, gram_pieces, hamil_pieces):
    nb = coefficients.shape[0]
    in_vmem = pl.BlockSpec(memory_space=pltpu.VMEM)
    result = jax.ShapeDtypeStruct(coefficients.shape, jnp.float32)
    square = pltpu.VMEM((nb, nb), jnp.float32)
    return pl.pallas_call(
        functools.partial(small_matrices, gram_pieces, hamil_pieces),
        out_shape=(result, result),
        in_specs=[pl.BlockSpec(memory_space=pltpu.SMEM), in_vmem, in_vmem],
        out_specs=(in_vmem, in_vmem),
        scratch_shapes=[square, square, pltpu.VMEM((EDGE, EDGE), jnp.float32)],
        cost_estimate=pl.CostEstimate(flops=2 * 10**10, bytes_accessed=2**22, transcendentals=0),
        compiler_params=pltpu.CompilerParams(vmem_limit_bytes=32 * 2**20),
    )(state, packed, coefficients)


def other_core(value):
    core, count = lax.axis_index("core"), value.shape[0] // 2
    kept = lax.dynamic_slice_in_dim(value, core * count, count, 0)
    sent = lax.dynamic_slice_in_dim(value, (1 - core) * count, count, 0)
    return kept + lax.ppermute(sent, "core", [(0, 1), (1, 0)])


def shards(x_block, h_block, mass_weights, coefficients):
    state = lax.axis_index("state")
    x_rows = lax.all_to_all(x_block, "state", 0, 1, tiled=True)
    points, nb = x_rows.shape
    h_rows = lax.all_to_all(after(h_block, x_rows), "state", 0, 1, tiled=True)
    gathered = lax.all_gather(after(x_block, h_rows), "state", axis=1, tiled=True)
    weights = lax.dynamic_slice_in_dim(mass_weights, state * points, points, 0)
    weighted_x = weights[:, None] * x_rows

    gram_firsts = [0 if EDGE * j < nb // 2 else nb // 2 for j in range(nb // EDGE)]
    hamil_firsts = [0] * (nb // EDGE)
    gram = other_core(pack(dot(x_rows, weighted_x, BY_COLS), gram_firsts))
    hamil = other_core(pack(dot(weighted_x, h_rows, BY_COLS), hamil_firsts))
    gram_rows, hamil_rows = gram.shape[0], hamil.shape[0]
    both = jnp.concatenate([gram, hamil], axis=0)
    both_rows = gram_rows + hamil_rows
    both = total(exchange(both, PLANE), PLANE)
    both = total(exchange(copies(both, LINE), LINE), LINE)
    both = exchange(copies(both, PLANE), PLANE)
    both = exchange(copies(both, "core"), "core")
    gram_splits = [(0, gram_rows, 0), (gram_rows, 2 * gram_rows, both_rows)]
    hamil_splits = [(0, hamil_rows, gram_rows), (hamil_rows, 2 * hamil_rows, both_rows + gram_rows)]
    rotation, projected = solve(
        state[None],
        both,
        coefficients,
        panel_pieces(gram_firsts, nb, gram_splits),
        panel_pieces(hamil_firsts, nb, hamil_splits),
    )
    rotated = jnp.dot(gathered, rotation, precision=lax.Precision.HIGH)
    return (rotated, projected)


def solution(mesh):
    split = Mesh(mesh.devices.reshape(4, 8, 2, 2, 4), ALL)
    placed = (P(GRID, "state"), P(GRID, "state"), P(GRID), P(None, "state"))
    return jax.shard_map(
        shards,
        mesh=split,
        in_specs=placed,
        out_specs=(P(GRID, "state"), P(None, "state")),
        check_vma=False,
    )
```

```python
import functools

import jax
import jax.numpy as jnp
from jax import lax
from jax.experimental import pallas as pl
from jax.experimental.pallas import tpu as pltpu
from jax.sharding import Mesh, PartitionSpec as P

GRID = ("x", "z", "yh", "core")
ALL = GRID + ("state",)
PLANE = ("x", "z")
LINE = ("yh", "state")
HIGHEST = lax.Precision.HIGHEST
EDGE, SUB, RUN = 128, 8, 16
dot = functools.partial(lax.dot_general, precision=HIGHEST, preferred_element_type=jnp.float32)
PLAIN, BY_ROWS, BY_COLS = (((1,), (0,)), ((), ())), (((1,), (1,)), ((), ())), (((0,), (0,)), ((), ()))


def after(value, *earlier):
    return lax.optimization_barrier((value, *earlier))[0]


def exchange(value, axes):
    return lax.all_to_all(value, axes, 0, 0, tiled=True)


def total(value, axes):
    return jnp.sum(value.reshape(lax.axis_size(axes), -1, value.shape[1]), axis=0)


def copies(value, axes):
    count = lax.axis_size(axes)
    return jnp.broadcast_to(value, (count,) + value.shape).reshape(-1, value.shape[1])


def block_inverse(rows):
    at_row = lax.broadcasted_iota(jnp.int32, (SUB, EDGE), 0)
    at_lane = lax.broadcasted_iota(jnp.int32, (SUB, EDGE), 1)
    groups = len(rows)
    left = list(rows)
    right = [jnp.where(at_lane == at_row + SUB * g, 1.0, 0.0).astype(jnp.float32) for g in range(groups)]

    def spread_row(value, c):
        return jnp.broadcast_to(value[c : c + 1, :], (SUB, EDGE))

    def spread_col(value, c):
        return jnp.broadcast_to(value[:, c : c + 1], (SUB, EDGE))

    for k in range(groups):
        cols = {g: [spread_col(left[g], SUB * k + c) for c in range(SUB)] for g in range(k, groups)}
        for c in range(SUB):
            scale = lax.rsqrt(spread_row(cols[k][c], c))
            inv = scale * scale
            left_row, right_row = spread_row(left[k], c), spread_row(right[k], c)
            col_row = {d: spread_row(cols[k][d], c) for d in range(c + 1, SUB)}
            below = jnp.where(at_row > c, cols[k][c], 0.0)
            for d in range(c + 1, SUB):
                cols[k][d] = cols[k][d] - (below * col_row[d]) * inv
            left[k] = left[k] - (below * left_row) * inv
            right[k] = jnp.where(at_row == c, right_row * scale, right[k] - (below * right_row) * inv)
            for g in range(k + 1, groups):
                factor = cols[g][c] * inv
                for d in range(c + 1, SUB):
                    cols[g][d] = cols[g][d] - factor * col_row[d]
                left[g] = left[g] - factor * left_row
                right[g] = right[g] - factor * right_row
    return right


def unpack(packed, states, matrix):
    nb = matrix.shape[0]
    for first in range(0, nb, RUN):
        for t in range(states):
            at = first * states + t * RUN
            matrix[first : first + RUN, EDGE * t : EDGE * (t + 1)] = packed[at : at + RUN, :]


def small_matrices(place_ref, own_packed, other_packed, coefficients, rotation_ref, projected_ref, work, hamil, inverse, block):
    nb = work.shape[0]
    blocks = nb // EDGE
    inverse[...] = jnp.zeros((nb, nb), jnp.float32)

    @pl.when(place_ref[0] == 0)
    def _():
        unpack(own_packed, blocks, work)
        unpack(other_packed, blocks, hamil)

    @pl.when(place_ref[0] != 0)
    def _():
        unpack(other_packed, blocks, work)
        unpack(own_packed, blocks, hamil)

    @pl.loop(0, blocks)
    def _(k):
        start = pl.multiple_of(k * EDGE, EDGE)
        rows = [
            work[pl.ds(pl.multiple_of(start + SUB * g, SUB), SUB), pl.ds(start, EDGE)]
            for g in range(EDGE // SUB)
        ]
        for g, row in enumerate(block_inverse(rows)):
            block[SUB * g : SUB * (g + 1), :] = row

        for j in range(blocks):

            @pl.when(k == j)
            def _():
                low, high = EDGE * j, EDGE * (j + 1)
                inverse[low:high, low:high] = block[...]
                if j + 1 < blocks:
                    panel = dot(work[high:, low:high], block[...], BY_ROWS)
                    work[high:, high:] = work[high:, high:] - dot(panel, panel, BY_ROWS)
                if j:
                    inverse[low:high, :low] = dot(block[...], inverse[low:high, :low], PLAIN)
                if j + 1 < blocks:
                    inverse[high:, :high] = inverse[high:, :high] - dot(panel, inverse[low:high, :high], PLAIN)

    for j in range(blocks):
        low, high = EDGE * j, EDGE * (j + 1)
        rotation_ref[low:high, :] = dot(inverse[low:, low:high], coefficients[low:, :], BY_COLS)
    own = pl.ds(pl.multiple_of(place_ref[1] * EDGE, EDGE), EDGE)
    half = dot(hamil[...], inverse[own, :], BY_ROWS)
    for j in range(blocks):
        high = EDGE * (j + 1)
        projected_ref[high - EDGE : high, :] = dot(inverse[high - EDGE : high, :high], half[:high], PLAIN)


def solve(place, own_packed, other_packed, coefficients):
    nb = coefficients.shape[0]
    in_vmem = pl.BlockSpec(memory_space=pltpu.VMEM)
    result = jax.ShapeDtypeStruct(coefficients.shape, jnp.float32)
    square = pltpu.VMEM((nb, nb), jnp.float32)
    return pl.pallas_call(
        small_matrices,
        out_shape=(result, result),
        in_specs=[pl.BlockSpec(memory_space=pltpu.SMEM), in_vmem, in_vmem, in_vmem],
        out_specs=(in_vmem, in_vmem),
        scratch_shapes=[square, square, square, pltpu.VMEM((EDGE, EDGE), jnp.float32)],
        cost_estimate=pl.CostEstimate(flops=2 * 10**10, bytes_accessed=2**22, transcendentals=0),
        compiler_params=pltpu.CompilerParams(vmem_limit_bytes=32 * 2**20),
    )(place, own_packed, other_packed, coefficients)


def high_low(value):
    high = value.astype(jnp.bfloat16)
    return high, (value - high.astype(jnp.float32)).astype(jnp.bfloat16)


def rotate_rows(source_ref, rotation_ref, *refs):
    *block_refs, rotated_ref = refs
    rows = [
        rotation_ref[pl.ds(pl.multiple_of(source_ref[b] * EDGE, EDGE), EDGE), :] for b in range(len(block_refs))
    ]
    turn_high, turn_low = high_low(jnp.concatenate(rows, axis=0))
    high, low = high_low(jnp.concatenate([ref[...] for ref in block_refs], axis=1))
    wide = jnp.dot(high, jnp.concatenate([turn_high, turn_low], axis=1), preferred_element_type=jnp.float32)
    small = wide[:, EDGE:] + jnp.dot(low, turn_high, preferred_element_type=jnp.float32)
    rotated_ref[...] = wide[:, :EDGE] + small


def rotate(sources, rotation, *blocks):
    rows, width = blocks[0].shape
    tile = rows // 4
    by_rows = pl.BlockSpec((tile, width), lambda i: (i, 0))
    return pl.pallas_call(
        rotate_rows,
        grid=(rows // tile,),
        out_shape=jax.ShapeDtypeStruct((rows, width), jnp.float32),
        in_specs=[
            pl.BlockSpec(memory_space=pltpu.SMEM),
            pl.BlockSpec(rotation.shape, lambda i: (0, 0)),
            *[by_rows] * len(blocks),
        ],
        out_specs=by_rows,
        cost_estimate=pl.CostEstimate(flops=2 * 10**9, bytes_accessed=6 * 2**20, transcendentals=0),
        compiler_params=pltpu.CompilerParams(vmem_limit_bytes=32 * 2**20),
    )(sources, rotation, *blocks)


def line_blocks(x_block, state):
    pairs = lax.ppermute(x_block, "state", [(0, 1), (1, 0), (2, 3), (3, 2)])
    middle = lax.ppermute(x_block, "state", [(1, 2), (2, 1)])
    outward = lax.ppermute(middle, "state", [(1, 0), (2, 3)])
    across = lax.ppermute(pairs, "state", [(1, 2), (2, 1)])
    far = lax.ppermute(across, "state", [(1, 0), (2, 3)])
    at_end = (state == 0) | (state == 3)
    return (
        (x_block, state),
        (pairs, state + 1 - 2 * (state % 2)),
        (jnp.where(at_end, outward, middle), jnp.where(state < 2, 2, 1)),
        (jnp.where(at_end, far, across), jnp.where(state < 2, 3, 0)),
    )


def shards(x_block, h_block, mass_weights, coefficients):
    state, core = lax.axis_index("state"), lax.axis_index("core")
    width = x_block.shape[1]
    blocks = line_blocks(x_block, state)
    weighted = mass_weights[:, None] * jnp.concatenate([x_block, h_block], axis=1)

    parts = jnp.zeros((2, len(blocks), width, width), jnp.float32)
    for block, source in blocks:
        product = dot(block, weighted, BY_COLS)
        product = jnp.stack([product[:, :width], product[:, width:]])
        parts = lax.dynamic_update_slice_in_dim(parts, product[:, None], source, 1)
    parts = parts.reshape(2, -1, width)

    kept = lax.dynamic_index_in_dim(parts, core, 0, keepdims=False)
    sent = lax.dynamic_index_in_dim(parts, 1 - core, 0, keepdims=False)
    summed = kept + lax.ppermute(sent, "core", [(0, 1), (1, 0)])
    summed = total(exchange(summed, PLANE), PLANE)
    summed = total(exchange(copies(summed, LINE), LINE), "yh")
    summed = exchange(copies(summed, PLANE), PLANE)
    other = lax.ppermute(summed, "core", [(0, 1), (1, 0)])
    rotation, projected = solve(jnp.stack([core, state]), summed, other, coefficients)
    rotated = rotate(jnp.stack([source for _, source in blocks]), rotation, *(block for block, _ in blocks))
    return (rotated, projected)


def solution(mesh):
    split = Mesh(mesh.devices.reshape(4, 8, 2, 2, 4), ALL)
    placed = (P(GRID, "state"), P(GRID, "state"), P(GRID), P(None, "state"))
    return jax.shard_map(
        shards,
        mesh=split,
        in_specs=placed,
        out_specs=(P(GRID, "state"), P(None, "state")),
        check_vma=False,
    )
```

```python
import functools

import jax
import jax.numpy as jnp
from jax import lax
from jax.experimental import pallas as pl
from jax.experimental.pallas import tpu as pltpu
from jax.sharding import Mesh, PartitionSpec as P

GRID = ("x", "z", "yh", "core")
ALL = GRID + ("state",)
PLANE = ("x", "z")
LINE = ("yh", "state")
HIGHEST = lax.Precision.HIGHEST
EDGE, SUB, RUN = 128, 8, 16
ROW_ORDER = ((1, 0, 2, 3), (2, 3, 1, 0))
dot = functools.partial(lax.dot_general, precision=HIGHEST, preferred_element_type=jnp.float32)
PLAIN, BY_ROWS, BY_COLS = (((1,), (0,)), ((), ())), (((1,), (1,)), ((), ())), (((0,), (0,)), ((), ()))


def after(value, *earlier):
    return lax.optimization_barrier((value, *earlier))[0]


def exchange(value, axes):
    return lax.all_to_all(value, axes, 0, 0, tiled=True)


def total(value, axes):
    return jnp.sum(value.reshape(lax.axis_size(axes), -1, value.shape[1]), axis=0)


def copies(value, axes):
    count = lax.axis_size(axes)
    return jnp.broadcast_to(value, (count,) + value.shape).reshape(-1, value.shape[1])


def block_inverse(rows):
    at_row = lax.broadcasted_iota(jnp.int32, (SUB, EDGE), 0)
    at_lane = lax.broadcasted_iota(jnp.int32, (SUB, EDGE), 1)
    groups = len(rows)
    left = list(rows)
    right = [jnp.where(at_lane == at_row + SUB * g, 1.0, 0.0).astype(jnp.float32) for g in range(groups)]

    def spread_row(value, c):
        return jnp.broadcast_to(value[c : c + 1, :], (SUB, EDGE))

    def spread_col(value, c):
        return jnp.broadcast_to(value[:, c : c + 1], (SUB, EDGE))

    for k in range(groups):
        cols = {g: [spread_col(left[g], SUB * k + c) for c in range(SUB)] for g in range(k, groups)}
        for c in range(SUB):
            scale = lax.rsqrt(spread_row(cols[k][c], c))
            inv = scale * scale
            left_row, right_row = spread_row(left[k], c), spread_row(right[k], c)
            col_row = {d: spread_row(cols[k][d], c) for d in range(c + 1, SUB)}
            below = jnp.where(at_row > c, cols[k][c], 0.0)
            for d in range(c + 1, SUB):
                cols[k][d] = cols[k][d] - (below * col_row[d]) * inv
            left[k] = left[k] - (below * left_row) * inv
            right[k] = jnp.where(at_row == c, right_row * scale, right[k] - (below * right_row) * inv)
            for g in range(k + 1, groups):
                factor = cols[g][c] * inv
                for d in range(c + 1, SUB):
                    cols[g][d] = cols[g][d] - factor * col_row[d]
                left[g] = left[g] - factor * left_row
                right[g] = right[g] - factor * right_row
    return right


def unpack(packed, matrix):
    panels = matrix.shape[1] // EDGE
    for run in range(matrix.shape[0] // RUN):
        for panel in range(panels):
            at = (run * panels + panel) * RUN
            first = ROW_ORDER[panel // 2][run * RUN // EDGE] * EDGE + run * RUN % EDGE
            matrix[first : first + RUN, EDGE * panel : EDGE * (panel + 1)] = packed[at : at + RUN, :]


def small_matrices(place_ref, own_packed, other_packed, coefficients, rotation_ref, projected_ref, work, hamil, inverse, block):
    nb = work.shape[0]
    blocks = nb // EDGE
    inverse[...] = jnp.zeros((nb, nb), jnp.float32)

    @pl.when(place_ref[0] == 0)
    def _():
        unpack(own_packed, work)
        unpack(other_packed, hamil)

    @pl.when(place_ref[0] != 0)
    def _():
        unpack(other_packed, work)
        unpack(own_packed, hamil)

    @pl.loop(0, blocks)
    def _(k):
        start = pl.multiple_of(k * EDGE, EDGE)
        rows = [
            work[pl.ds(pl.multiple_of(start + SUB * g, SUB), SUB), pl.ds(start, EDGE)]
            for g in range(EDGE // SUB)
        ]
        for g, row in enumerate(block_inverse(rows)):
            block[SUB * g : SUB * (g + 1), :] = row

        for j in range(blocks):

            @pl.when(k == j)
            def _():
                low, high = EDGE * j, EDGE * (j + 1)
                inverse[low:high, low:high] = block[...]
                if j + 1 < blocks:
                    panel = dot(work[high:, low:high], block[...], BY_ROWS)
                    work[high:, high:] = work[high:, high:] - dot(panel, panel, BY_ROWS)
                if j:
                    inverse[low:high, :low] = dot(block[...], inverse[low:high, :low], PLAIN)
                if j + 1 < blocks:
                    inverse[high:, :high] = inverse[high:, :high] - dot(panel, inverse[low:high, :high], PLAIN)

    for j in range(blocks):
        low, high = EDGE * j, EDGE * (j + 1)
        rotation_ref[low:high, :] = dot(inverse[low:, low:high], coefficients[low:, :], BY_COLS)
    own = pl.ds(pl.multiple_of(place_ref[1] * EDGE, EDGE), EDGE)
    half = dot(hamil[...], inverse[own, :], BY_ROWS)
    for j in range(blocks):
        high = EDGE * (j + 1)
        projected_ref[high - EDGE : high, :] = dot(inverse[high - EDGE : high, :high], half[:high], PLAIN)


def solve(place, own_packed, other_packed, coefficients):
    nb = coefficients.shape[0]
    in_vmem = pl.BlockSpec(memory_space=pltpu.VMEM)
    result = jax.ShapeDtypeStruct(coefficients.shape, jnp.float32)
    square = pltpu.VMEM((nb, nb), jnp.float32)
    return pl.pallas_call(
        small_matrices,
        out_shape=(result, result),
        in_specs=[pl.BlockSpec(memory_space=pltpu.SMEM), in_vmem, in_vmem, in_vmem],
        out_specs=(in_vmem, in_vmem),
        scratch_shapes=[square, square, square, pltpu.VMEM((EDGE, EDGE), jnp.float32)],
        cost_estimate=pl.CostEstimate(flops=2 * 10**10, bytes_accessed=2**22, transcendentals=0),
        compiler_params=pltpu.CompilerParams(vmem_limit_bytes=32 * 2**20),
    )(place, own_packed, other_packed, coefficients)


def high_low(value):
    high = value.astype(jnp.bfloat16)
    return high, (value - high.astype(jnp.float32)).astype(jnp.bfloat16)


def rotate_rows(source_ref, rotation_ref, own, pairs, middle, outward, across, far, rotated_ref):
    rows = [rotation_ref[pl.ds(pl.multiple_of(source_ref[b] * EDGE, EDGE), EDGE), :] for b in range(4)]
    turn_high, turn_low = high_low(jnp.concatenate(rows, axis=0))
    at_end = source_ref[4] == 1
    third, fourth = jnp.where(at_end, outward[...], middle[...]), jnp.where(at_end, far[...], across[...])
    high, low = high_low(jnp.concatenate([own[...], pairs[...], third, fourth], axis=1))
    wide = jnp.dot(high, jnp.concatenate([turn_high, turn_low], axis=1), preferred_element_type=jnp.float32)
    small = wide[:, EDGE:] + jnp.dot(low, turn_high, preferred_element_type=jnp.float32)
    rotated_ref[...] = wide[:, :EDGE] + small


def rotate(state, rotation, *blocks):
    rows, width = blocks[0].shape
    tile = rows // 4
    by_rows = pl.BlockSpec((tile, width), lambda i: (i, 0))
    at_end = (state == 0) | (state == 3)
    sources = [
        state,
        state + 1 - 2 * (state % 2),
        jnp.where(state < 2, 2, 1),
        jnp.where(state < 2, 3, 0),
        at_end.astype(jnp.int32),
    ]
    return pl.pallas_call(
        rotate_rows,
        grid=(rows // tile,),
        out_shape=jax.ShapeDtypeStruct((rows, width), jnp.float32),
        in_specs=[
            pl.BlockSpec(memory_space=pltpu.SMEM),
            pl.BlockSpec(rotation.shape, lambda i: (0, 0)),
            *[by_rows] * len(blocks),
        ],
        out_specs=by_rows,
        cost_estimate=pl.CostEstimate(flops=2 * 10**9, bytes_accessed=8 * 2**20, transcendentals=0),
        compiler_params=pltpu.CompilerParams(vmem_limit_bytes=32 * 2**20),
    )(jnp.stack(sources), rotation, *blocks)


def shards(x_block, h_block, mass_weights, coefficients):
    state, core = lax.axis_index("state"), lax.axis_index("core")
    width = x_block.shape[1]
    send = functools.partial(lax.ppermute, axis_name="state")

    pairs = send(x_block, perm=[(0, 1), (1, 0), (2, 3), (3, 2)])
    middle = send(x_block, perm=[(1, 2), (2, 1)])
    across = send(pairs, perm=[(1, 2), (2, 1)])
    outer_h = send(after(h_block, pairs), perm=[(0, 1), (3, 2)])
    outward = send(middle, perm=[(1, 0), (2, 3)])
    far = send(across, perm=[(1, 0), (2, 3)])
    times = functools.partial(
        lax.dot_general,
        dimension_numbers=BY_COLS,
        precision=lax.Precision.HIGH,
        preferred_element_type=jnp.float32,
    )
    near = jnp.concatenate([x_block, pairs, middle], axis=1)
    early = mass_weights[:, None] * jnp.concatenate([pairs, x_block, h_block], axis=1)
    late = mass_weights[:, None] * outer_h
    near_early, near_late = times(near, early), times(near, late)
    far_early, far_late = times(across, early), times(across, late)
    gram = jnp.concatenate([near_early[:, : 2 * width], far_early[:, : 2 * width]], axis=0)
    hamil_outer = jnp.concatenate([near_late, far_late], axis=0)
    hamil_own = jnp.concatenate([near_early[:, 2 * width :], far_early[:, 2 * width :]], axis=0)
    hamil = jnp.concatenate([hamil_outer, hamil_own], axis=1)

    kept, sent = jnp.where(core == 0, gram, hamil), jnp.where(core == 0, hamil, gram)
    summed = kept + lax.ppermute(sent, "core", [(0, 1), (1, 0)])
    summed = total(exchange(after(summed, outward), PLANE), PLANE)
    summed = after(summed, far)
    shape = (lax.axis_size("yh"), lax.axis_size("state")) + summed.shape
    summed = jnp.sum(exchange(copies(summed, LINE), LINE).reshape(shape), axis=0)
    panels = summed[1][:, :width], summed[1][:, width:], summed[2][:, width:], summed[2][:, :width]
    summed = exchange(copies(jnp.concatenate(panels, axis=0), PLANE), PLANE)
    other = lax.ppermute(summed, "core", [(0, 1), (1, 0)])
    rotation, projected = solve(jnp.stack([core, state]), summed, other, coefficients)
    rotated = rotate(state, rotation, x_block, pairs, middle, outward, across, far)
    return (rotated, projected)


def solution(mesh):
    split = Mesh(mesh.devices.reshape(4, 8, 2, 2, 4), ALL)
    placed = (P(GRID, "state"), P(GRID, "state"), P(GRID), P(None, "state"))
    return jax.shard_map(
        shards,
        mesh=split,
        in_specs=placed,
        out_specs=(P(GRID, "state"), P(None, "state")),
        check_vma=False,
    )
```

```python
import functools

import jax
import jax.numpy as jnp
from jax import lax
from jax.experimental import pallas as pl
from jax.experimental.pallas import tpu as pltpu
from jax.sharding import Mesh, PartitionSpec as P

GRID = ("x", "z", "yh", "core")
ALL = GRID + ("state",)
PLANE = ("x", "z")
LINE = ("yh", "state")
HIGHEST = lax.Precision.HIGHEST
EDGE, SUB, RUN = 128, 8, 16
ROW_ORDER = ((1, 0, 2, 3), (2, 3, 1, 0))
dot = functools.partial(lax.dot_general, precision=HIGHEST, preferred_element_type=jnp.float32)
PLAIN, BY_ROWS, BY_COLS = (((1,), (0,)), ((), ())), (((1,), (1,)), ((), ())), (((0,), (0,)), ((), ()))


def after(value, *earlier):
    return lax.optimization_barrier((value, *earlier))[0]


def exchange(value, axes):
    return lax.all_to_all(value, axes, 0, 0, tiled=True)


def total(value, axes):
    return jnp.sum(value.reshape(lax.axis_size(axes), -1, value.shape[1]), axis=0)


def copies(value, axes):
    count = lax.axis_size(axes)
    return jnp.broadcast_to(value, (count,) + value.shape).reshape(-1, value.shape[1])


def block_inverse(rows):
    at_row = lax.broadcasted_iota(jnp.int32, (SUB, EDGE), 0)
    at_lane = lax.broadcasted_iota(jnp.int32, (SUB, EDGE), 1)
    groups = len(rows)
    left = list(rows)
    right = [jnp.where(at_lane == at_row + SUB * g, 1.0, 0.0).astype(jnp.float32) for g in range(groups)]

    def spread_row(value, c):
        return jnp.broadcast_to(value[c : c + 1, :], (SUB, EDGE))

    def spread_col(value, c):
        return jnp.broadcast_to(value[:, c : c + 1], (SUB, EDGE))

    for k in range(groups):
        cols = {g: [spread_col(left[g], SUB * k + c) for c in range(SUB)] for g in range(k, groups)}
        for c in range(SUB):
            scale = lax.rsqrt(spread_row(cols[k][c], c))
            inv = scale * scale
            left_row, right_row = spread_row(left[k], c), spread_row(right[k], c)
            col_row = {d: spread_row(cols[k][d], c) for d in range(c + 1, SUB)}
            below = jnp.where(at_row > c, cols[k][c], 0.0)
            for d in range(c + 1, SUB):
                cols[k][d] = cols[k][d] - (below * col_row[d]) * inv
            left[k] = left[k] - (below * left_row) * inv
            right[k] = jnp.where(at_row == c, right_row * scale, right[k] - (below * right_row) * inv)
            for g in range(k + 1, groups):
                factor = cols[g][c] * inv
                for d in range(c + 1, SUB):
                    cols[g][d] = cols[g][d] - factor * col_row[d]
                left[g] = left[g] - factor * left_row
                right[g] = right[g] - factor * right_row
    return right


def unpack(packed, matrix):
    panels = matrix.shape[1] // EDGE
    for run in range(matrix.shape[0] // RUN):
        for panel in range(panels):
            at = (run * panels + panel) * RUN
            first = ROW_ORDER[panel // 2][run * RUN // EDGE] * EDGE + run * RUN % EDGE
            matrix[first : first + RUN, EDGE * panel : EDGE * (panel + 1)] = packed[at : at + RUN, :]


def small_matrices(place_ref, own_packed, other_packed, coefficients, rotation_ref, projected_ref, work, hamil, inverse, block):
    nb = work.shape[0]
    blocks = nb // EDGE
    inverse[...] = jnp.zeros((nb, nb), jnp.float32)

    @pl.when(place_ref[0] == 0)
    def _():
        unpack(own_packed, work)
        unpack(other_packed, hamil)

    @pl.when(place_ref[0] != 0)
    def _():
        unpack(other_packed, work)
        unpack(own_packed, hamil)

    @pl.loop(0, blocks)
    def _(k):
        start = pl.multiple_of(k * EDGE, EDGE)
        rows = [
            work[pl.ds(pl.multiple_of(start + SUB * g, SUB), SUB), pl.ds(start, EDGE)]
            for g in range(EDGE // SUB)
        ]
        for g, row in enumerate(block_inverse(rows)):
            block[SUB * g : SUB * (g + 1), :] = row

        for j in range(blocks):

            @pl.when(k == j)
            def _():
                low, high = EDGE * j, EDGE * (j + 1)
                inverse[low:high, low:high] = block[...]
                if j + 1 < blocks:
                    panel = dot(work[high:, low:high], block[...], BY_ROWS)
                    work[high:, high:] = work[high:, high:] - dot(panel, panel, BY_ROWS)
                if j:
                    inverse[low:high, :low] = dot(block[...], inverse[low:high, :low], PLAIN)
                if j + 1 < blocks:
                    inverse[high:, :high] = inverse[high:, :high] - dot(panel, inverse[low:high, :high], PLAIN)

    for j in range(blocks):
        low, high = EDGE * j, EDGE * (j + 1)
        rotation_ref[low:high, :] = dot(inverse[low:, low:high], coefficients[low:, :], BY_COLS)
    own = pl.ds(pl.multiple_of(place_ref[1] * EDGE, EDGE), EDGE)
    half = dot(hamil[...], inverse[own, :], BY_ROWS)
    for j in range(blocks):
        high = EDGE * (j + 1)
        projected_ref[high - EDGE : high, :] = dot(inverse[high - EDGE : high, :high], half[:high], PLAIN)


def solve(place, own_packed, other_packed, coefficients):
    nb = coefficients.shape[0]
    in_vmem = pl.BlockSpec(memory_space=pltpu.VMEM)
    result = jax.ShapeDtypeStruct(coefficients.shape, jnp.float32)
    square = pltpu.VMEM((nb, nb), jnp.float32)
    return pl.pallas_call(
        small_matrices,
        out_shape=(result, result),
        in_specs=[pl.BlockSpec(memory_space=pltpu.SMEM), in_vmem, in_vmem, in_vmem],
        out_specs=(in_vmem, in_vmem),
        scratch_shapes=[square, square, square, pltpu.VMEM((EDGE, EDGE), jnp.float32)],
        cost_estimate=pl.CostEstimate(flops=2 * 10**10, bytes_accessed=2**22, transcendentals=0),
        compiler_params=pltpu.CompilerParams(vmem_limit_bytes=32 * 2**20),
    )(place, own_packed, other_packed, coefficients)


def high_low(value):
    high = value.astype(jnp.bfloat16)
    return high, (value - high.astype(jnp.float32)).astype(jnp.bfloat16)


def rotate_rows(source_ref, rotation_ref, own, pairs, middle, outward, across, far, rotated_ref):
    rows = [rotation_ref[pl.ds(pl.multiple_of(source_ref[b] * EDGE, EDGE), EDGE), :] for b in range(4)]
    turn_high, turn_low = high_low(jnp.concatenate(rows, axis=0))
    at_end = source_ref[4] == 1
    third, fourth = jnp.where(at_end, outward[...], middle[...]), jnp.where(at_end, far[...], across[...])
    high, low = high_low(jnp.concatenate([own[...], pairs[...], third, fourth], axis=1))
    wide = jnp.dot(high, jnp.concatenate([turn_high, turn_low], axis=1), preferred_element_type=jnp.float32)
    small = wide[:, EDGE:] + jnp.dot(low, turn_high, preferred_element_type=jnp.float32)
    rotated_ref[...] = wide[:, :EDGE] + small


def rotate(state, rotation, *blocks):
    rows, width = blocks[0].shape
    tile = rows // 4
    by_rows = pl.BlockSpec((tile, width), lambda i: (i, 0))
    at_end = (state == 0) | (state == 3)
    sources = [
        state,
        state + 1 - 2 * (state % 2),
        jnp.where(state < 2, 2, 1),
        jnp.where(state < 2, 3, 0),
        at_end.astype(jnp.int32),
    ]
    return pl.pallas_call(
        rotate_rows,
        grid=(rows // tile,),
        out_shape=jax.ShapeDtypeStruct((rows, width), jnp.float32),
        in_specs=[
            pl.BlockSpec(memory_space=pltpu.SMEM),
            pl.BlockSpec(rotation.shape, lambda i: (0, 0)),
            *[by_rows] * len(blocks),
        ],
        out_specs=by_rows,
        cost_estimate=pl.CostEstimate(flops=2 * 10**9, bytes_accessed=8 * 2**20, transcendentals=0),
        compiler_params=pltpu.CompilerParams(vmem_limit_bytes=32 * 2**20),
    )(jnp.stack(sources), rotation, *blocks)


def shards(x_block, h_block, mass_weights, coefficients):
    state, core = lax.axis_index("state"), lax.axis_index("core")
    width = x_block.shape[1]
    send = functools.partial(lax.ppermute, axis_name="state")

    pairs = send(x_block, perm=[(0, 1), (1, 0), (2, 3), (3, 2)])
    middle = send(x_block, perm=[(1, 2), (2, 1)])
    outer_h = send(h_block, perm=[(0, 1), (3, 2)])
    across = send(pairs, perm=[(1, 2), (2, 1)])
    outward = send(middle, perm=[(1, 0), (2, 3)])
    far = send(across, perm=[(1, 0), (2, 3)])
    times = functools.partial(
        lax.dot_general,
        dimension_numbers=BY_COLS,
        precision=lax.Precision.HIGH,
        preferred_element_type=jnp.float32,
    )
    near = jnp.concatenate([x_block, pairs, middle], axis=1)
    weighted = mass_weights[:, None] * jnp.concatenate([pairs, x_block, outer_h, h_block], axis=1)
    products = jnp.concatenate([times(near, weighted), times(across, weighted)], axis=0)
    gram, hamil = products[:, : 2 * width], products[:, 2 * width :]

    kept, sent = jnp.where(core == 0, gram, hamil), jnp.where(core == 0, hamil, gram)
    summed = kept + lax.ppermute(sent, "core", [(0, 1), (1, 0)])
    summed = total(exchange(after(summed, outward), PLANE), PLANE)
    summed = after(summed, far)
    shape = (lax.axis_size("yh"), lax.axis_size("state")) + summed.shape
    summed = jnp.sum(exchange(copies(summed, LINE), LINE).reshape(shape), axis=0)
    panels = summed[1][:, :width], summed[1][:, width:], summed[2][:, width:], summed[2][:, :width]
    summed = exchange(copies(jnp.concatenate(panels, axis=0), PLANE), PLANE)
    other = lax.ppermute(summed, "core", [(0, 1), (1, 0)])
    rotation, projected = solve(jnp.stack([core, state]), summed, other, coefficients)
    rotated = rotate(state, rotation, x_block, pairs, middle, outward, across, far)
    return (rotated, projected)


def solution(mesh):
    split = Mesh(mesh.devices.reshape(4, 8, 2, 2, 4), ALL)
    placed = (P(GRID, "state"), P(GRID, "state"), P(GRID), P(None, "state"))
    return jax.shard_map(
        shards,
        mesh=split,
        in_specs=placed,
        out_specs=(P(GRID, "state"), P(None, "state")),
        check_vma=False,
    )
```

```python
import functools

import jax
import jax.numpy as jnp
from jax import lax
from jax.experimental import pallas as pl
from jax.experimental.pallas import tpu as pltpu
from jax.sharding import Mesh, PartitionSpec as P

GRID = ("x", "z", "yh", "core")
ALL = GRID + ("state",)
PLANE = ("x", "z")
LINE = ("yh", "state")
HIGHEST = lax.Precision.HIGHEST
EDGE, SUB, RUN = 128, 8, 16
ROW_ORDER = ((1, 0, 2, 3), (2, 3, 1, 0))
dot = functools.partial(lax.dot_general, precision=HIGHEST, preferred_element_type=jnp.float32)
PLAIN, BY_ROWS, BY_COLS = (((1,), (0,)), ((), ())), (((1,), (1,)), ((), ())), (((0,), (0,)), ((), ()))


def after(value, *earlier):
    return lax.optimization_barrier((value, *earlier))[0]


def exchange(value, axes):
    return lax.all_to_all(value, axes, 0, 0, tiled=True)


def total(value, axes):
    return jnp.sum(value.reshape(lax.axis_size(axes), -1, value.shape[1]), axis=0)


def copies(value, axes):
    count = lax.axis_size(axes)
    return jnp.broadcast_to(value, (count,) + value.shape).reshape(-1, value.shape[1])


def block_inverse(rows):
    at_row = lax.broadcasted_iota(jnp.int32, (SUB, EDGE), 0)
    at_lane = lax.broadcasted_iota(jnp.int32, (SUB, EDGE), 1)
    groups = len(rows)
    left = list(rows)
    right = [jnp.where(at_lane == at_row + SUB * g, 1.0, 0.0).astype(jnp.float32) for g in range(groups)]

    def spread_row(value, c):
        return jnp.broadcast_to(value[c : c + 1, :], (SUB, EDGE))

    def spread_col(value, c):
        return jnp.broadcast_to(value[:, c : c + 1], (SUB, EDGE))

    for k in range(groups):
        cols = {g: [spread_col(left[g], SUB * k + c) for c in range(SUB)] for g in range(k, groups)}
        for c in range(SUB):
            scale = lax.rsqrt(spread_row(cols[k][c], c))
            inv = scale * scale
            left_row, right_row = spread_row(left[k], c), spread_row(right[k], c)
            col_row = {d: spread_row(cols[k][d], c) for d in range(c + 1, SUB)}
            below = jnp.where(at_row > c, cols[k][c], 0.0)
            for d in range(c + 1, SUB):
                cols[k][d] = cols[k][d] - (below * col_row[d]) * inv
            left[k] = left[k] - (below * left_row) * inv
            right[k] = jnp.where(at_row == c, right_row * scale, right[k] - (below * right_row) * inv)
            for g in range(k + 1, groups):
                factor = cols[g][c] * inv
                for d in range(c + 1, SUB):
                    cols[g][d] = cols[g][d] - factor * col_row[d]
                left[g] = left[g] - factor * left_row
                right[g] = right[g] - factor * right_row
    return right


def unpack(packed, matrix):
    panels = matrix.shape[1] // EDGE
    for run in range(matrix.shape[0] // RUN):
        for panel in range(panels):
            at = (run * panels + panel) * RUN
            first = ROW_ORDER[panel // 2][run * RUN // EDGE] * EDGE + run * RUN % EDGE
            matrix[first : first + RUN, EDGE * panel : EDGE * (panel + 1)] = packed[at : at + RUN, :]


def small_matrices(place_ref, own_packed, other_packed, coefficients, rotation_ref, projected_ref, work, hamil, inverse, block):
    nb = work.shape[0]
    blocks = nb // EDGE
    inverse[...] = jnp.zeros((nb, nb), jnp.float32)

    @pl.when(place_ref[0] == 0)
    def _():
        unpack(own_packed, work)
        unpack(other_packed, hamil)

    @pl.when(place_ref[0] != 0)
    def _():
        unpack(other_packed, work)
        unpack(own_packed, hamil)

    @pl.loop(0, blocks)
    def _(k):
        start = pl.multiple_of(k * EDGE, EDGE)
        rows = [
            work[pl.ds(pl.multiple_of(start + SUB * g, SUB), SUB), pl.ds(start, EDGE)]
            for g in range(EDGE // SUB)
        ]
        for g, row in enumerate(block_inverse(rows)):
            block[SUB * g : SUB * (g + 1), :] = row

        for j in range(blocks):

            @pl.when(k == j)
            def _():
                low, high = EDGE * j, EDGE * (j + 1)
                inverse[low:high, low:high] = block[...]
                if j + 1 < blocks:
                    panel = dot(work[high:, low:high], block[...], BY_ROWS)
                    work[high:, high:] = work[high:, high:] - dot(panel, panel, BY_ROWS)
                if j:
                    inverse[low:high, :low] = dot(block[...], inverse[low:high, :low], PLAIN)
                if j + 1 < blocks:
                    inverse[high:, :high] = inverse[high:, :high] - dot(panel, inverse[low:high, :high], PLAIN)

    for j in range(blocks):
        low, high = EDGE * j, EDGE * (j + 1)
        rotation_ref[low:high, :] = dot(inverse[low:, low:high], coefficients[low:, :], BY_COLS)
    own = pl.ds(pl.multiple_of(place_ref[1] * EDGE, EDGE), EDGE)
    half = dot(hamil[...], inverse[own, :], BY_ROWS)
    for j in range(blocks):
        high = EDGE * (j + 1)
        projected_ref[high - EDGE : high, :] = dot(inverse[high - EDGE : high, :high], half[:high], PLAIN)


def solve(place, own_packed, other_packed, coefficients):
    nb = coefficients.shape[0]
    in_vmem = pl.BlockSpec(memory_space=pltpu.VMEM)
    result = jax.ShapeDtypeStruct(coefficients.shape, jnp.float32)
    square = pltpu.VMEM((nb, nb), jnp.float32)
    return pl.pallas_call(
        small_matrices,
        out_shape=(result, result),
        in_specs=[pl.BlockSpec(memory_space=pltpu.SMEM), in_vmem, in_vmem, in_vmem],
        out_specs=(in_vmem, in_vmem),
        scratch_shapes=[square, square, square, pltpu.VMEM((EDGE, EDGE), jnp.float32)],
        cost_estimate=pl.CostEstimate(flops=2 * 10**10, bytes_accessed=2**22, transcendentals=0),
        compiler_params=pltpu.CompilerParams(vmem_limit_bytes=32 * 2**20),
    )(place, own_packed, other_packed, coefficients)


def high_low(value):
    high = value.astype(jnp.bfloat16)
    return high, (value - high.astype(jnp.float32)).astype(jnp.bfloat16)


def rotate_rows(source_ref, rotation_ref, own, pairs, middle, outward, across, far, rotated_ref):
    rows = [rotation_ref[pl.ds(pl.multiple_of(source_ref[b] * EDGE, EDGE), EDGE), :] for b in range(4)]
    turn_high, turn_low = high_low(jnp.concatenate(rows, axis=0))
    at_end = source_ref[4] == 1
    third, fourth = jnp.where(at_end, outward[...], middle[...]), jnp.where(at_end, far[...], across[...])
    high, low = high_low(jnp.concatenate([own[...], pairs[...], third, fourth], axis=1))
    wide = jnp.dot(high, jnp.concatenate([turn_high, turn_low], axis=1), preferred_element_type=jnp.float32)
    small = wide[:, EDGE:] + jnp.dot(low, turn_high, preferred_element_type=jnp.float32)
    rotated_ref[...] = wide[:, :EDGE] + small


def rotate(state, rotation, *blocks):
    rows, width = blocks[0].shape
    tile = rows // 4
    by_rows = pl.BlockSpec((tile, width), lambda i: (i, 0))
    at_end = (state == 0) | (state == 3)
    sources = [
        state,
        state + 1 - 2 * (state % 2),
        jnp.where(state < 2, 2, 1),
        jnp.where(state < 2, 3, 0),
        at_end.astype(jnp.int32),
    ]
    return pl.pallas_call(
        rotate_rows,
        grid=(rows // tile,),
        out_shape=jax.ShapeDtypeStruct((rows, width), jnp.float32),
        in_specs=[
            pl.BlockSpec(memory_space=pltpu.SMEM),
            pl.BlockSpec(rotation.shape, lambda i: (0, 0)),
            *[by_rows] * len(blocks),
        ],
        out_specs=by_rows,
        cost_estimate=pl.CostEstimate(flops=2 * 10**9, bytes_accessed=8 * 2**20, transcendentals=0),
        compiler_params=pltpu.CompilerParams(vmem_limit_bytes=32 * 2**20),
    )(jnp.stack(sources), rotation, *blocks)


def shards(x_block, h_block, mass_weights, coefficients):
    state, core = lax.axis_index("state"), lax.axis_index("core")
    width = x_block.shape[1]
    send = functools.partial(lax.ppermute, axis_name="state")

    pairs = send(x_block, perm=[(0, 1), (1, 0), (2, 3), (3, 2)])
    middle = send(x_block, perm=[(1, 2), (2, 1)])
    outer_h = send(h_block, perm=[(0, 1), (3, 2)])
    across = send(pairs, perm=[(1, 2), (2, 1)])
    outward = send(middle, perm=[(1, 0), (2, 3)])
    far = send(across, perm=[(1, 0), (2, 3)])
    times = functools.partial(
        lax.dot_general,
        dimension_numbers=BY_COLS,
        precision=lax.Precision.HIGH,
        preferred_element_type=jnp.float32,
    )
    near = jnp.concatenate([x_block, pairs, middle], axis=1)
    early = mass_weights[:, None] * jnp.concatenate([pairs, x_block, h_block], axis=1)
    near_early = times(near, early)
    outer_h, last = after((outer_h, across), near_early)
    late = mass_weights[:, None] * outer_h
    near_late = times(near, late)
    far_all = times(last, jnp.concatenate([early, late], axis=1))
    gram = jnp.concatenate([near_early[:, : 2 * width], far_all[:, : 2 * width]], axis=0)
    hamil_outer = jnp.concatenate([near_late, far_all[:, 3 * width :]], axis=0)
    hamil_own = jnp.concatenate([near_early[:, 2 * width :], far_all[:, 2 * width : 3 * width]], axis=0)
    hamil = jnp.concatenate([hamil_outer, hamil_own], axis=1)

    kept, sent = jnp.where(core == 0, gram, hamil), jnp.where(core == 0, hamil, gram)
    summed = kept + lax.ppermute(sent, "core", [(0, 1), (1, 0)])
    summed = total(exchange(after(summed, outward), PLANE), PLANE)
    shape = (lax.axis_size("yh"), lax.axis_size("state")) + summed.shape
    summed = jnp.sum(exchange(copies(summed, LINE), LINE).reshape(shape), axis=0)
    panels = summed[1][:, :width], summed[1][:, width:], summed[2][:, width:], summed[2][:, :width]
    summed = exchange(copies(jnp.concatenate(panels, axis=0), PLANE), PLANE)
    other = lax.ppermute(after(summed, far), "core", [(0, 1), (1, 0)])
    rotation, projected = solve(jnp.stack([core, state]), summed, other, coefficients)
    rotated = rotate(state, rotation, x_block, pairs, middle, outward, across, far)
    return (rotated, projected)


def solution(mesh):
    split = Mesh(mesh.devices.reshape(4, 8, 2, 2, 4), ALL)
    placed = (P(GRID, "state"), P(GRID, "state"), P(GRID), P(None, "state"))
    return jax.shard_map(
        shards,
        mesh=split,
        in_specs=placed,
        out_specs=(P(GRID, "state"), P(None, "state")),
        check_vma=False,
    )
```

```python
import functools

import jax
import jax.numpy as jnp
from jax import lax
from jax.experimental import pallas as pl
from jax.experimental.pallas import tpu as pltpu
from jax.sharding import Mesh, PartitionSpec as P

GRID = ("x", "z", "yh", "core")
ALL = GRID + ("state",)
PLANE = ("x", "z")
LINE = ("yh", "state")
HIGHEST = lax.Precision.HIGHEST
EDGE, SUB, RUN = 128, 8, 16
ROW_ORDER = ((1, 0, 2, 3), (2, 3, 1, 0))
dot = functools.partial(lax.dot_general, precision=HIGHEST, preferred_element_type=jnp.float32)
PLAIN, BY_ROWS, BY_COLS = (((1,), (0,)), ((), ())), (((1,), (1,)), ((), ())), (((0,), (0,)), ((), ()))


def after(value, *earlier):
    return lax.optimization_barrier((value, *earlier))[0]


def exchange(value, axes):
    return lax.all_to_all(value, axes, 0, 0, tiled=True)


def total(value, axes):
    return jnp.sum(value.reshape(lax.axis_size(axes), -1, value.shape[1]), axis=0)


def copies(value, axes):
    count = lax.axis_size(axes)
    return jnp.broadcast_to(value, (count,) + value.shape).reshape(-1, value.shape[1])


def block_inverse(rows):
    at_row = lax.broadcasted_iota(jnp.int32, (SUB, EDGE), 0)
    at_lane = lax.broadcasted_iota(jnp.int32, (SUB, EDGE), 1)
    groups = len(rows)
    left = list(rows)
    right = [jnp.where(at_lane == at_row + SUB * g, 1.0, 0.0).astype(jnp.float32) for g in range(groups)]

    def spread_row(value, c):
        return jnp.broadcast_to(value[c : c + 1, :], (SUB, EDGE))

    def spread_col(value, c):
        return jnp.broadcast_to(value[:, c : c + 1], (SUB, EDGE))

    for k in range(groups):
        cols = {g: [spread_col(left[g], SUB * k + c) for c in range(SUB)] for g in range(k, groups)}
        for c in range(SUB):
            scale = lax.rsqrt(spread_row(cols[k][c], c))
            inv = scale * scale
            left_row, right_row = spread_row(left[k], c), spread_row(right[k], c)
            col_row = {d: spread_row(cols[k][d], c) for d in range(c + 1, SUB)}
            below = jnp.where(at_row > c, cols[k][c], 0.0)
            for d in range(c + 1, SUB):
                cols[k][d] = cols[k][d] - (below * col_row[d]) * inv
            left[k] = left[k] - (below * left_row) * inv
            right[k] = jnp.where(at_row == c, right_row * scale, right[k] - (below * right_row) * inv)
            for g in range(k + 1, groups):
                factor = cols[g][c] * inv
                for d in range(c + 1, SUB):
                    cols[g][d] = cols[g][d] - factor * col_row[d]
                left[g] = left[g] - factor * left_row
                right[g] = right[g] - factor * right_row
    return right


def unpack(place_ref, own, other, matrix):
    def place(arrays):
        for run in range(matrix.shape[0] // RUN):
            for panel in range(matrix.shape[1] // EDGE):
                at = (2 * run + panel // 2) * RUN
                first = ROW_ORDER[panel // 2][run * RUN // EDGE] * EDGE + run * RUN % EDGE
                rows = arrays[panel in (1, 2)][at : at + RUN, :]
                matrix[first : first + RUN, EDGE * panel : EDGE * (panel + 1)] = rows

    @pl.when(place_ref[0] == 0)
    def _():
        place((own, other))

    @pl.when(place_ref[0] != 0)
    def _():
        place((other, own))


def factor_kernel(place_ref, own, other, coefficients, rotation_ref, inverse, work, block):
    nb = work.shape[0]
    blocks = nb // EDGE
    inverse[...] = jnp.zeros((nb, nb), jnp.float32)
    unpack(place_ref, own, other, work)

    @pl.loop(0, blocks)
    def _(k):
        start = pl.multiple_of(k * EDGE, EDGE)
        rows = [
            work[pl.ds(pl.multiple_of(start + SUB * g, SUB), SUB), pl.ds(start, EDGE)]
            for g in range(EDGE // SUB)
        ]
        for g, row in enumerate(block_inverse(rows)):
            block[SUB * g : SUB * (g + 1), :] = row

        for j in range(blocks):

            @pl.when(k == j)
            def _():
                low, high = EDGE * j, EDGE * (j + 1)
                inverse[low:high, low:high] = block[...]
                if j + 1 < blocks:
                    panel = dot(work[high:, low:high], block[...], BY_ROWS)
                    work[high:, high:] = work[high:, high:] - dot(panel, panel, BY_ROWS)
                if j:
                    inverse[low:high, :low] = dot(block[...], inverse[low:high, :low], PLAIN)
                if j + 1 < blocks:
                    inverse[high:, :high] = inverse[high:, :high] - dot(panel, inverse[low:high, :high], PLAIN)

    for j in range(blocks):
        low, high = EDGE * j, EDGE * (j + 1)
        rotation_ref[low:high, :] = dot(inverse[low:, low:high], coefficients[low:, :], BY_COLS)

def project_kernel(place_ref, own, other, inverse, projected_ref, hamil):
    unpack(place_ref, own, other, hamil)
    rows = pl.ds(pl.multiple_of(place_ref[1] * EDGE, EDGE), EDGE)
    half = dot(hamil[...], inverse[rows, :], BY_ROWS)
    for j in range(hamil.shape[0] // EDGE):
        high = EDGE * (j + 1)
        projected_ref[high - EDGE : high, :] = dot(inverse[high - EDGE : high, :high], half[:high], PLAIN)


def in_vmem(kernel, out_shape, scratch_shapes, flops, place, *arrays):
    spec = pl.BlockSpec(memory_space=pltpu.VMEM)
    return pl.pallas_call(
        kernel,
        out_shape=out_shape,
        in_specs=[pl.BlockSpec(memory_space=pltpu.SMEM)] + [spec] * len(arrays),
        out_specs=jax.tree.map(lambda _: spec, out_shape),
        scratch_shapes=scratch_shapes,
        cost_estimate=pl.CostEstimate(flops=flops, bytes_accessed=2**22, transcendentals=0),
        compiler_params=pltpu.CompilerParams(vmem_limit_bytes=16 * 2**20),
    )(place, *arrays)


def factor(place, own, other, coefficients):
    nb, width = coefficients.shape
    outs = jax.ShapeDtypeStruct((nb, width), jnp.float32), jax.ShapeDtypeStruct((nb, nb), jnp.float32)
    scratch = [pltpu.VMEM((nb, nb), jnp.float32), pltpu.VMEM((EDGE, EDGE), jnp.float32)]
    return in_vmem(factor_kernel, outs, scratch, 2 * 10**10, place, own, other, coefficients)


def project(place, own, other, inverse):
    nb = inverse.shape[0]
    out = jax.ShapeDtypeStruct((nb, EDGE), jnp.float32)
    return in_vmem(project_kernel, out, [pltpu.VMEM((nb, nb), jnp.float32)], 10**9, place, own, other, inverse)


def high_low(value):
    high = value.astype(jnp.bfloat16)
    return high, (value - high.astype(jnp.float32)).astype(jnp.bfloat16)


def rotate_rows(source_ref, rotation_ref, own, pairs, middle, outward, across, far, rotated_ref):
    rows = [rotation_ref[pl.ds(pl.multiple_of(source_ref[b] * EDGE, EDGE), EDGE), :] for b in range(4)]
    turn_high, turn_low = high_low(jnp.concatenate(rows, axis=0))
    at_end = source_ref[4] == 1
    third, fourth = jnp.where(at_end, outward[...], middle[...]), jnp.where(at_end, far[...], across[...])
    high, low = high_low(jnp.concatenate([own[...], pairs[...], third, fourth], axis=1))
    wide = jnp.dot(high, jnp.concatenate([turn_high, turn_low], axis=1), preferred_element_type=jnp.float32)
    small = wide[:, EDGE:] + jnp.dot(low, turn_high, preferred_element_type=jnp.float32)
    rotated_ref[...] = wide[:, :EDGE] + small


def rotate(state, rotation, *blocks):
    rows, width = blocks[0].shape
    tile = rows // 4
    by_rows = pl.BlockSpec((tile, width), lambda i: (i, 0))
    at_end = (state == 0) | (state == 3)
    sources = [
        state,
        state + 1 - 2 * (state % 2),
        jnp.where(state < 2, 2, 1),
        jnp.where(state < 2, 3, 0),
        at_end.astype(jnp.int32),
    ]
    return pl.pallas_call(
        rotate_rows,
        grid=(rows // tile,),
        out_shape=jax.ShapeDtypeStruct((rows, width), jnp.float32),
        in_specs=[
            pl.BlockSpec(memory_space=pltpu.SMEM),
            pl.BlockSpec(rotation.shape, lambda i: (0, 0)),
            *[by_rows] * len(blocks),
        ],
        out_specs=by_rows,
        cost_estimate=pl.CostEstimate(flops=2 * 10**9, bytes_accessed=8 * 2**20, transcendentals=0),
        compiler_params=pltpu.CompilerParams(vmem_limit_bytes=16 * 2**20),
    )(jnp.stack(sources), rotation, *blocks)


def shards(x_block, h_block, mass_weights, coefficients):
    state, core = lax.axis_index("state"), lax.axis_index("core")
    width = x_block.shape[1]
    send = functools.partial(lax.ppermute, axis_name="state")

    pairs = send(x_block, perm=[(0, 1), (1, 0), (2, 3), (3, 2)])
    middle = send(x_block, perm=[(1, 2), (2, 1)])
    outer_h = send(h_block, perm=[(0, 1), (3, 2)])
    across = send(pairs, perm=[(1, 2), (2, 1)])
    outward = send(middle, perm=[(1, 0), (2, 3)])
    far = send(across, perm=[(1, 0), (2, 3)])
    times = functools.partial(
        lax.dot_general,
        dimension_numbers=BY_COLS,
        precision=lax.Precision.HIGH,
        preferred_element_type=jnp.float32,
    )
    near = jnp.concatenate([x_block, pairs, middle], axis=1)
    early = mass_weights[:, None] * jnp.concatenate([pairs, x_block, h_block], axis=1)
    near_early = times(near, early)
    outer_h, last = after((outer_h, across), near_early)
    late = mass_weights[:, None] * outer_h
    near_late = times(near, late)
    far_all = times(last, jnp.concatenate([early, late], axis=1))
    gram = jnp.concatenate([near_early[:, : 2 * width], far_all[:, : 2 * width]], axis=0)
    hamil_outer = jnp.concatenate([near_late, far_all[:, 3 * width :]], axis=0)
    hamil_own = jnp.concatenate([near_early[:, 2 * width :], far_all[:, 2 * width : 3 * width]], axis=0)
    hamil = jnp.concatenate([hamil_outer, hamil_own], axis=1)

    outer = jnp.concatenate([gram[:, :width], hamil[:, :width]], axis=1)
    inner = jnp.concatenate([gram[:, width:], hamil[:, width:]], axis=1)
    kept, sent = jnp.where(core == 0, outer, inner), jnp.where(core == 0, inner, outer)
    swap = functools.partial(lax.ppermute, axis_name="core", perm=[(0, 1), (1, 0)])
    summed = kept + swap(sent)
    summed = total(exchange(after(summed, outward), PLANE), PLANE)
    shape = (lax.axis_size("yh"), lax.axis_size("state")) + summed.shape
    summed = jnp.sum(exchange(copies(summed, LINE), LINE).reshape(shape), axis=0)[1:3].reshape(-1, 2 * width)
    gram, hamil = summed[:, :width], summed[:, width:]
    gram = exchange(copies(gram, PLANE), PLANE)
    hamil = exchange(copies(after(hamil, gram), PLANE), PLANE)
    place = jnp.stack([core, state])
    rotation, inverse = factor(place, gram, swap(gram), coefficients)
    hamil = after(hamil, rotation)
    rotated = rotate(state, rotation, x_block, pairs, middle, outward, across, far)
    projected = project(place, hamil, swap(hamil), inverse)
    return (rotated, projected)


def solution(mesh):
    split = Mesh(mesh.devices.reshape(4, 8, 2, 2, 4), ALL)
    placed = (P(GRID, "state"), P(GRID, "state"), P(GRID), P(None, "state"))
    return jax.shard_map(
        shards,
        mesh=split,
        in_specs=placed,
        out_specs=(P(GRID, "state"), P(None, "state")),
        check_vma=False,
    )
```

```python
import functools

import jax
import jax.numpy as jnp
from jax import lax
from jax.experimental import pallas as pl
from jax.experimental.pallas import tpu as pltpu
from jax.sharding import Mesh, PartitionSpec as P

GRID = ("x", "z", "yh", "core")
ALL = GRID + ("state",)
PLANE = ("x", "z")
LINE = ("yh", "state")
HIGHEST = lax.Precision.HIGHEST
EDGE, SUB, RUN = 128, 8, 16
ROW_ORDER = ((1, 0, 2, 3), (2, 3, 1, 0))
dot = functools.partial(lax.dot_general, precision=HIGHEST, preferred_element_type=jnp.float32)
PLAIN, BY_ROWS, BY_COLS = (((1,), (0,)), ((), ())), (((1,), (1,)), ((), ())), (((0,), (0,)), ((), ()))


def after(value, *earlier):
    return lax.optimization_barrier((value, *earlier))[0]


def exchange(value, axes):
    return lax.all_to_all(value, axes, 0, 0, tiled=True)


def total(value, axes):
    return jnp.sum(value.reshape(lax.axis_size(axes), -1, value.shape[1]), axis=0)


def copies(value, axes):
    count = lax.axis_size(axes)
    return jnp.broadcast_to(value, (count,) + value.shape).reshape(-1, value.shape[1])


def block_inverse(rows):
    at_row = lax.broadcasted_iota(jnp.int32, (SUB, EDGE), 0)
    at_lane = lax.broadcasted_iota(jnp.int32, (SUB, EDGE), 1)
    groups = len(rows)
    left = list(rows)
    right = [jnp.where(at_lane == at_row + SUB * g, 1.0, 0.0).astype(jnp.float32) for g in range(groups)]

    def spread_row(value, c):
        return jnp.broadcast_to(value[c : c + 1, :], (SUB, EDGE))

    def spread_col(value, c):
        return jnp.broadcast_to(value[:, c : c + 1], (SUB, EDGE))

    for k in range(groups):
        cols = {g: [spread_col(left[g], SUB * k + c) for c in range(SUB)] for g in range(k, groups)}
        for c in range(SUB):
            scale = lax.rsqrt(spread_row(cols[k][c], c))
            inv = scale * scale
            left_row, right_row = spread_row(left[k], c), spread_row(right[k], c)
            col_row = {d: spread_row(cols[k][d], c) for d in range(c + 1, SUB)}
            below = jnp.where(at_row > c, cols[k][c], 0.0)
            for d in range(c + 1, SUB):
                cols[k][d] = cols[k][d] - (below * col_row[d]) * inv
            left[k] = left[k] - (below * left_row) * inv
            right[k] = jnp.where(at_row == c, right_row * scale, right[k] - (below * right_row) * inv)
            for g in range(k + 1, groups):
                factor = cols[g][c] * inv
                for d in range(c + 1, SUB):
                    cols[g][d] = cols[g][d] - factor * col_row[d]
                left[g] = left[g] - factor * left_row
                right[g] = right[g] - factor * right_row
    return right


def high_low(value):
    high = value.astype(jnp.bfloat16)
    return high, (value - high.astype(jnp.float32)).astype(jnp.bfloat16)


def three_products(left, right, numbers):
    (left_high, left_low), (right_high, right_low) = high_low(left), high_low(right)
    times = functools.partial(lax.dot_general, dimension_numbers=numbers, preferred_element_type=jnp.float32)
    return times(left_high, right_high) + (times(left_high, right_low) + times(left_low, right_high))


def unpack(packed, matrix):
    panels = matrix.shape[1] // EDGE
    for run in range(matrix.shape[0] // RUN):
        for panel in range(panels):
            at = (run * panels + panel) * RUN
            first = ROW_ORDER[panel // 2][run * RUN // EDGE] * EDGE + run * RUN % EDGE
            matrix[first : first + RUN, EDGE * panel : EDGE * (panel + 1)] = packed[at : at + RUN, :]


def small_matrices(place_ref, own_packed, other_packed, coefficients, rotation_ref, projected_ref, work, hamil, inverse, block):
    nb = work.shape[0]
    blocks = nb // EDGE
    inverse[...] = jnp.zeros((nb, nb), jnp.float32)

    @pl.when(place_ref[0] == 0)
    def _():
        unpack(own_packed, work)
        unpack(other_packed, hamil)

    @pl.when(place_ref[0] != 0)
    def _():
        unpack(other_packed, work)
        unpack(own_packed, hamil)

    @pl.loop(0, blocks)
    def _(k):
        start = pl.multiple_of(k * EDGE, EDGE)
        rows = [
            work[pl.ds(pl.multiple_of(start + SUB * g, SUB), SUB), pl.ds(start, EDGE)]
            for g in range(EDGE // SUB)
        ]
        for g, row in enumerate(block_inverse(rows)):
            block[SUB * g : SUB * (g + 1), :] = row

        for j in range(blocks):

            @pl.when(k == j)
            def _():
                low, high = EDGE * j, EDGE * (j + 1)
                inverse[low:high, low:high] = block[...]
                if j + 1 < blocks:
                    panel = dot(work[high:, low:high], block[...], BY_ROWS)
                    work[high:, high:] = work[high:, high:] - dot(panel, panel, BY_ROWS)
                if j:
                    inverse[low:high, :low] = dot(block[...], inverse[low:high, :low], PLAIN)
                if j + 1 < blocks:
                    inverse[high:, :high] = inverse[high:, :high] - dot(panel, inverse[low:high, :high], PLAIN)

    for j in range(blocks):
        low, high = EDGE * j, EDGE * (j + 1)
        rotation_ref[low:high, :] = dot(inverse[low:, low:high], coefficients[low:, :], BY_COLS)
    own = pl.ds(pl.multiple_of(place_ref[1] * EDGE, EDGE), EDGE)
    half = three_products(hamil[...], inverse[own, :], BY_ROWS)
    for j in range(blocks):
        high = EDGE * (j + 1)
        projected_ref[high - EDGE : high, :] = three_products(inverse[high - EDGE : high, :high], half[:high], PLAIN)


def solve(place, own_packed, other_packed, coefficients):
    nb = coefficients.shape[0]
    in_vmem = pl.BlockSpec(memory_space=pltpu.VMEM)
    result = jax.ShapeDtypeStruct(coefficients.shape, jnp.float32)
    square = pltpu.VMEM((nb, nb), jnp.float32)
    return pl.pallas_call(
        small_matrices,
        out_shape=(result, result),
        in_specs=[pl.BlockSpec(memory_space=pltpu.SMEM), in_vmem, in_vmem, in_vmem],
        out_specs=(in_vmem, in_vmem),
        scratch_shapes=[square, square, square, pltpu.VMEM((EDGE, EDGE), jnp.float32)],
        cost_estimate=pl.CostEstimate(flops=2 * 10**10, bytes_accessed=2**22, transcendentals=0),
        compiler_params=pltpu.CompilerParams(vmem_limit_bytes=32 * 2**20),
    )(place, own_packed, other_packed, coefficients)


def rotate_rows(source_ref, rotation_ref, own, pairs, middle, outward, across, far, rotated_ref):
    rows = [rotation_ref[pl.ds(pl.multiple_of(source_ref[b] * EDGE, EDGE), EDGE), :] for b in range(4)]
    turn_high, turn_low = high_low(jnp.concatenate(rows, axis=0))
    at_end = source_ref[4] == 1
    third, fourth = jnp.where(at_end, outward[...], middle[...]), jnp.where(at_end, far[...], across[...])
    high, low = high_low(jnp.concatenate([own[...], pairs[...], third, fourth], axis=1))
    wide = jnp.dot(high, jnp.concatenate([turn_high, turn_low], axis=1), preferred_element_type=jnp.float32)
    small = wide[:, EDGE:] + jnp.dot(low, turn_high, preferred_element_type=jnp.float32)
    rotated_ref[...] = wide[:, :EDGE] + small


def rotate(state, rotation, *blocks):
    rows, width = blocks[0].shape
    tile = rows // 4
    by_rows = pl.BlockSpec((tile, width), lambda i: (i, 0))
    at_end = (state == 0) | (state == 3)
    sources = [
        state,
        state + 1 - 2 * (state % 2),
        jnp.where(state < 2, 2, 1),
        jnp.where(state < 2, 3, 0),
        at_end.astype(jnp.int32),
    ]
    return pl.pallas_call(
        rotate_rows,
        grid=(rows // tile,),
        out_shape=jax.ShapeDtypeStruct((rows, width), jnp.float32),
        in_specs=[
            pl.BlockSpec(memory_space=pltpu.SMEM),
            pl.BlockSpec(rotation.shape, lambda i: (0, 0)),
            *[by_rows] * len(blocks),
        ],
        out_specs=by_rows,
        cost_estimate=pl.CostEstimate(flops=2 * 10**9, bytes_accessed=8 * 2**20, transcendentals=0),
        compiler_params=pltpu.CompilerParams(vmem_limit_bytes=32 * 2**20),
    )(jnp.stack(sources), rotation, *blocks)


def shards(x_block, h_block, mass_weights, coefficients):
    state, core = lax.axis_index("state"), lax.axis_index("core")
    width = x_block.shape[1]
    send = functools.partial(lax.ppermute, axis_name="state")

    pairs = send(x_block, perm=[(0, 1), (1, 0), (2, 3), (3, 2)])
    middle = send(x_block, perm=[(1, 2), (2, 1)])
    outer_h = send(h_block, perm=[(0, 1), (3, 2)])
    across = send(pairs, perm=[(1, 2), (2, 1)])
    outward = send(middle, perm=[(1, 0), (2, 3)])
    far = send(across, perm=[(1, 0), (2, 3)])
    times = functools.partial(
        lax.dot_general,
        dimension_numbers=BY_COLS,
        precision=lax.Precision.HIGH,
        preferred_element_type=jnp.float32,
    )
    near = jnp.concatenate([x_block, pairs, middle], axis=1)
    weighted = mass_weights[:, None] * jnp.concatenate([pairs, x_block, outer_h, h_block], axis=1)
    products = jnp.concatenate([times(near, weighted), times(across, weighted)], axis=0)
    gram, hamil = products[:, : 2 * width], products[:, 2 * width :]

    kept, sent = jnp.where(core == 0, gram, hamil), jnp.where(core == 0, hamil, gram)
    summed = kept + lax.ppermute(sent, "core", [(0, 1), (1, 0)])
    summed = total(exchange(after(summed, outward), PLANE), PLANE)
    shape = (lax.axis_size("yh"), lax.axis_size("state")) + summed.shape
    summed = jnp.sum(exchange(copies(summed, LINE), LINE).reshape(shape), axis=0)
    panels = summed[1][:, :width], summed[1][:, width:], summed[2][:, width:], summed[2][:, :width]
    summed = exchange(copies(jnp.concatenate(panels, axis=0), PLANE), PLANE)
    other = lax.ppermute(summed, "core", [(0, 1), (1, 0)])
    rotation, projected = solve(jnp.stack([core, state]), summed, other, coefficients)
    rotated = rotate(state, rotation, x_block, pairs, middle, outward, across, far)
    return (rotated, projected)


def solution(mesh):
    split = Mesh(mesh.devices.reshape(4, 8, 2, 2, 4), ALL)
    placed = (P(GRID, "state"), P(GRID, "state"), P(GRID), P(None, "state"))
    return jax.shard_map(
        shards,
        mesh=split,
        in_specs=placed,
        out_specs=(P(GRID, "state"), P(None, "state")),
        check_vma=False,
    )
```
